32 devices in a mesh: parts: 2 (over x), dp: 4 (over y, core), tensor: 4 (over z).
Axes of the slice: x: 2, y: 2, z: 4, core: 2. Of those that a mesh axis runs over, the one named last changes fastest.
Arguments:
- hidden_input_rows: bfloat16 [10240, 28672], P(('parts', 'dp'), 'tensor'), parts along dimension 0, may hold values from -6 to 6
- output_gradient_rows: bfloat16 [10240, 8192], P(('parts', 'dp'), 'tensor'), parts along dimension 0, may hold values from -6 to 6
- adapter_down_matrix: bfloat16 [16, 28672], P(None, 'tensor'), may hold values from -0.03125 to 0.03125
- input_side_projection: bfloat16 [64, 28672], P(None, 'tensor'), may hold values from -0.03125 to 0.03125
- adapter_up_matrix: bfloat16 [8192, 16], P('tensor'), may hold values from -0.0625 to 0.0625
- output_side_projection: bfloat16 [64, 8192], P(None, 'tensor'), may hold values from -0.0625 to 0.0625
- projected_test_gradients: bfloat16 [4096, 2048], P('dp', 'tensor'), may hold values from -0.0078125 to 0.0078125
Outputs:
- scores: float32 [40, 4096], P(('parts', 'dp'), 'tensor'), parts along dimension 0
The draws below stay inside these ranges and needn't reach their ends.
There are 2 independent parts, one for each index of `parts`. The reference program is written for one: setup_inputs(seed, part) draws one part's arguments, and reference() takes and returns one part's arrays. A program takes and returns all parts, laid end to end along the dimension named above; an argument that names none is the same for every part. Nothing has to cross between parts.
All inputs are finite; a program needn't handle non-finite values.
Results may differ from the reference program's by a relative error of at most 0.0029.
Values may be sent and summed in bfloat16 or wider, within the bound.
A program may use at most 128 MiB of HBM per device.

```python
import jax
import jax.numpy as jnp
from jax import lax

MODEL_WIDTH = 8192
HIDDEN_UNITS = 28672
ADAPTER_RANK = 16
KDIM = 64
LEN = 256
GRAD = 2048
TOKENS = 5120
TEST = 4096


def shard_levels(own_key, shape, pieces, least, top_value):
    factor_of = 1.0
    for axis_at, blocks in pieces:
        draws = jax.random.uniform(jax.random.fold_in(jax.random.fold_in(own_key, 6), axis_at), (blocks,), jnp.float32, least / len(pieces), top_value / len(pieces))
        factor_of = factor_of * jnp.repeat(jnp.exp(draws), shape[axis_at] // blocks).reshape((-1,) + (1,) * (len(shape) - 1 - axis_at))
    return factor_of


def normal_values(stream_key, dims, spread, most, shards=(), kind=jnp.bfloat16):
    result = spread * jax.random.normal(stream_key, dims, jnp.float32)
    if shards:
        result = result * shard_levels(stream_key, dims, shards, -0.22, 0.18)
    return jnp.clip(result, -most, most).astype(kind)


def setup_inputs(seed: int = 0, part: int = 0) -> dict:
    arg_keys = jax.random.split(jax.random.key(seed), 8)
    own_keys = jax.random.split(jax.random.fold_in(arg_keys[7], part), 8)
    return {
        "hidden_input_rows": normal_values(own_keys[0], (TOKENS, HIDDEN_UNITS), 1.0, 6.0, ((0, 4), (1, 4))),
        "output_gradient_rows": normal_values(own_keys[1], (TOKENS, MODEL_WIDTH), 1.0, 6.0, ((0, 4), (1, 4))),
        "adapter_down_matrix": normal_values(arg_keys[2], (ADAPTER_RANK, HIDDEN_UNITS), HIDDEN_UNITS ** -0.5, 0.03125, ((1, 4),)),
        "input_side_projection": normal_values(arg_keys[3], (KDIM, HIDDEN_UNITS), HIDDEN_UNITS ** -0.5, 0.03125, ((1, 4),)),
        "adapter_up_matrix": normal_values(arg_keys[4], (MODEL_WIDTH, ADAPTER_RANK), MODEL_WIDTH ** -0.5, 0.0625, ((0, 4),)),
        "output_side_projection": normal_values(arg_keys[5], (KDIM, MODEL_WIDTH), MODEL_WIDTH ** -0.5, 0.0625, ((1, 4),)),
        "projected_test_gradients": normal_values(arg_keys[6], (TEST, GRAD), (2 * ADAPTER_RANK * KDIM * LEN) ** -0.5, 0.0078125, ((0, 4), (1, 4))),
    }


def reference(hidden_input_rows, output_gradient_rows, adapter_down_matrix, input_side_projection, adapter_up_matrix, output_side_projection, projected_test_gradients):
    contract = (((1,), (1,)), ((), ()))
    left_factor = jnp.concatenate([adapter_down_matrix, input_side_projection], 0)
    right_factor = jnp.concatenate([adapter_up_matrix.T, output_side_projection], 0)
    input_side = lax.dot_general(hidden_input_rows, left_factor, contract, preferred_element_type=jnp.float32)
    grad_side = lax.dot_general(output_gradient_rows, right_factor, contract, preferred_element_type=jnp.float32)
    seqs = TOKENS // LEN
    u_part = input_side[:, :ADAPTER_RANK].reshape(seqs, LEN, ADAPTER_RANK)
    x_part = input_side[:, ADAPTER_RANK:].reshape(seqs, LEN, KDIM)
    v_part = grad_side[:, :ADAPTER_RANK].reshape(seqs, LEN, ADAPTER_RANK)
    g_part = grad_side[:, ADAPTER_RANK:].reshape(seqs, LEN, KDIM)
    grad_b = jnp.einsum('slk,slr->skr', g_part, u_part, precision=lax.Precision.HIGHEST)
    grad_a = jnp.einsum('slr,slk->srk', v_part, x_part, precision=lax.Precision.HIGHEST)
    example = jnp.concatenate([grad_b.reshape(seqs, -1), grad_a.reshape(seqs, -1)], 1).astype(jnp.bfloat16)
    return lax.dot_general(example, projected_test_gradients, contract, preferred_element_type=jnp.float32)
```

```python
import functools

import jax
import jax.numpy as jnp
from jax import lax
from jax.experimental import pallas as pl
from jax.experimental.pallas import tpu as pltpu
from jax.sharding import PartitionSpec as P

LEN = 256
MESH = pl.DeviceIdType.MESH
WIRE = jnp.bfloat16
CONTRACT_LAST = (((1,), (1,)), ((), ()))
CONTRACT_FIRST = (((0,), (0,)), ((), ()))


def split(x):
    high = x.astype(jnp.bfloat16)
    return jnp.concatenate([high, (x - high.astype(jnp.float32)).astype(jnp.bfloat16)], 0)


def kernel(
    sizes,
    hidden, outgrad, down, inproj, up_t, outproj, tests,
    out,
    hid_v, grad_v, left_v, right_v, tests_v,
    own_a, own_b, send_p, recv_p, own_e, recv_e, own_s, all_s, part_s, recv_s,
    hid_sem, grad_sem, w_sem, t_sem,
    p_send, p_recv, e_send, e_recv, s_send, s_recv, o_send, o_recv,
):
    nd, nt = sizes
    rank, kdim = down.shape[0], inproj.shape[0]
    seqs = hidden.shape[0] // LEN
    block = LEN // nt
    pack = min(4, block // 16)
    width = tests.shape[1]
    rep = kdim // rank
    f32, bf16 = jnp.float32, jnp.bfloat16

    part = lax.axis_index("parts")
    d = lax.axis_index("dp")
    t = lax.axis_index("tensor")

    loads = []

    def load(src, dst, sem):
        copy = pltpu.make_async_copy(src, dst, sem)
        copy.start()
        return copy

    w_loads = [load(inproj, left_v.at[pl.ds(0, kdim)], w_sem.at[0])]
    for i in range(rep):
        w_loads.append(load(down, left_v.at[pl.ds(kdim + rank * i, rank)], w_sem.at[1 + i]))
    hid_loads, grad_loads = [], []
    for s in range(seqs):
        rows = pl.ds(s * LEN, LEN)
        hid_loads.append(load(hidden.at[rows], hid_v.at[rows], hid_sem.at[s]))
        if s == 0:
            for i in range(rep):
                w_loads.append(load(up_t, right_v.at[pl.ds(rank * i, rank)], w_sem.at[1 + rep + i]))
            w_loads.append(load(outproj, right_v.at[pl.ds(kdim, kdim)], w_sem.at[1 + 2 * rep]))
        grad_loads.append(load(outgrad.at[rows], grad_v.at[rows], grad_sem.at[s]))
    t_load = load(tests, tests_v, t_sem)

    barrier = pltpu.get_barrier_semaphore()
    for kd in range(nd):
        for kt in range(nt):
            if kd or kt:
                pl.semaphore_signal(
                    barrier, inc=1,
                    device_id=(part, lax.rem(d + kd, nd), lax.rem(t + kt, nt)),
                    device_id_type=MESH,
                )

    lane = lax.broadcasted_iota(jnp.int32, (LEN, 2 * kdim), 1)
    low = lane < kdim
    lane16 = lax.broadcasted_iota(jnp.int32, (16, 2 * kdim), 1)
    group = (lane16 // rank) % rep

    p_copies, e_copies = [], []

    def project(s):
        rows = pl.ds(s * LEN, LEN)
        hid_loads[s].wait()
        if s == 0:
            for c in w_loads[:1 + rep]:
                c.wait()
        from_in = lax.dot_general(hid_v[rows, :], left_v[...], CONTRACT_LAST, preferred_element_type=f32)
        grad_loads[s].wait()
        if s == 0:
            for c in w_loads[1 + rep:]:
                c.wait()
        from_gr = lax.dot_general(grad_v[rows, :], right_v[...], CONTRACT_LAST, preferred_element_type=f32)
        a = jnp.where(low, from_in, from_gr)
        b = jnp.where(low, from_gr, from_in)
        own_a[s] = a
        for j in range(nt):
            at = j * block
            packed = jnp.zeros((16, 2 * kdim), f32)
            for i in range(pack):
                packed = jnp.where(group == i, b[at + 16 * i:at + 16 * i + 16], packed)
            own_b[s, j] = packed
            send_p[s, j, pl.ds(0, block), :] = a[at:at + block].astype(WIRE)
            packed_hi = packed.astype(WIRE)
            send_p[s, j, pl.ds(block, 16), :] = packed_hi
            send_p[s, j, pl.ds(block + 16, 16), :] = (packed - packed_hi.astype(f32)).astype(WIRE)
        if s == 0:
            pl.semaphore_wait(barrier, nd * nt - 1)
        copies = []
        for k in range(1, nt):
            to = lax.rem(t + k, nt)
            c = pltpu.make_async_remote_copy(
                src_ref=send_p.at[s, to], dst_ref=recv_p.at[s, k - 1],
                send_sem=p_send.at[s, k - 1], recv_sem=p_recv.at[s, k - 1],
                device_id=(part, d, to), device_id_type=MESH,
            )
            c.start()
            copies.append(c)
        p_copies.append(copies)

    def bilinear(s):
        for c in p_copies[s]:
            c.wait_recv()
        a = own_a[s, pl.ds(pl.multiple_of(t * block, block), block), :]
        b = own_b[s, t]
        for k in range(nt - 1):
            a = a + recv_p[s, k, pl.ds(0, block), :].astype(f32)
            b = b + recv_p[s, k, pl.ds(block, 16), :].astype(f32)
            b = b + recv_p[s, k, pl.ds(block + 16, 16), :].astype(f32)
        b = jnp.concatenate([jnp.where(group == i, b, 0.0) for i in range(pack)], 0)
        a_hi, b_hi = a.astype(bf16), b.astype(bf16)
        a_lo = (a - a_hi.astype(f32)).astype(bf16)
        b_lo = (b - b_hi.astype(f32)).astype(bf16)
        z = lax.dot_general(
            jnp.concatenate([b_hi, b_lo, b_hi], 0), jnp.concatenate([a_hi, a_hi, a_lo], 0),
            CONTRACT_FIRST, preferred_element_type=f32,
        )
        va, ub = z[0:rank], z[kdim:kdim + rank]
        for i in range(1, pack):
            va = va + z[rank * i:rank * i + rank]
            ub = ub + z[kdim + rank * i:kdim + rank * i + rank]
        own_e[s] = jnp.where(lane16 < kdim, va, ub)
        copies = []
        for k in range(1, nt):
            to = lax.rem(t + k, nt)
            c = pltpu.make_async_remote_copy(
                src_ref=own_e.at[s], dst_ref=recv_e.at[k - 1, s],
                send_sem=e_send.at[s, k - 1], recv_sem=e_recv.at[s, k - 1],
                device_id=(part, d, to), device_id_type=MESH,
            )
            c.start()
            copies.append(c)
        e_copies.append(copies)

    for s in range(seqs):
        project(s)
        if s >= 2:
            bilinear(s - 2)
    for s in range(max(seqs - 2, 0), seqs):
        bilinear(s)

    half = rank * kdim
    rows_e = 2 * seqs * rank
    col = lax.broadcasted_iota(jnp.int32, (2 * kdim, width), 1) + t * width
    lane_of = jnp.where(col < half, kdim + col // rank, (col - half) % kdim)
    pick = (lax.broadcasted_iota(jnp.int32, (2 * kdim, width), 0) == lane_of).astype(bf16)
    colr = lax.broadcasted_iota(jnp.int32, (rows_e, width), 1) + t * width
    row_of = jnp.where(colr < half, colr % rank, (colr - half) // kdim)
    keep = (lax.broadcasted_iota(jnp.int32, (rows_e, width), 0) % rank) == row_of
    fold = (
        (lax.broadcasted_iota(jnp.int32, (8, rows_e), 1) // rank) % seqs
        == lax.broadcasted_iota(jnp.int32, (8, rows_e), 0)
    ).astype(bf16)

    for copies in e_copies:
        for c in copies:
            c.wait_recv()
    e = own_e[...]
    for k in range(nt - 1):
        e = e + recv_e[k]
    e = split(e.reshape(seqs * rank, 2 * kdim))
    spread = jnp.dot(e, pick, preferred_element_type=f32)
    spread = jnp.where(keep, spread, 0.0).astype(bf16)
    example = jnp.dot(fold, spread, preferred_element_type=f32)
    own_s[...] = example
    s_copies = []
    for k in range(1, nd):
        c = pltpu.make_async_remote_copy(
            src_ref=own_s, dst_ref=all_s.at[k - 1],
            send_sem=s_send.at[k - 1], recv_sem=s_recv.at[k - 1],
            device_id=(part, lax.rem(d + k, nd), t), device_id_type=MESH,
        )
        c.start()
        s_copies.append(c)
    t_load.wait()

    for c in s_copies:
        c.wait_recv()
    stacked = split(jnp.concatenate([example] + [all_s[k] for k in range(nd - 1)], 0))
    scores = lax.dot_general(stacked, tests_v[...], CONTRACT_LAST, preferred_element_type=f32)
    scores = scores[:8 * nd] + scores[8 * nd:]
    per = nd // nt
    home = d // per
    slot = lax.rem(d, per)
    part_s[...] = scores.reshape(part_s.shape)

    def send_scores(k):
        to = lax.rem(d + nd - k, nd)
        return pltpu.make_async_remote_copy(
            src_ref=part_s.at[k], dst_ref=recv_s.at[slot, t],
            send_sem=o_send.at[k], recv_sem=o_recv.at[slot, t],
            device_id=(part, to, home), device_id_type=MESH,
        )

    for k in range(nd):
        if k == 0:
            @pl.when(home != t)
            def _():
                send_scores(0).start()

            @pl.when(home == t)
            def _():
                recv_s[slot, t] = part_s[0]
        else:
            send_scores(k).start()

    for j in range(per):
        total = None
        for i in range(nt):
            local = jnp.logical_and(t * per + j == d, i == t)

            @pl.when(jnp.logical_not(local))
            def _():
                pltpu.make_async_remote_copy(
                    src_ref=part_s.at[0], dst_ref=recv_s.at[j, i],
                    send_sem=o_send.at[0], recv_sem=o_recv.at[j, i],
                    device_id=(part, d, t), device_id_type=MESH,
                ).wait_recv()
            total = recv_s[j, i] if total is None else total + recv_s[j, i]
        tests_here = tests.shape[0]
        out[:, j * tests_here:(j + 1) * tests_here] = total[:seqs]

    for copies in p_copies + e_copies + [s_copies]:
        for c in copies:
            c.wait_send()
    for k in range(nd):
        if k == 0:
            @pl.when(home != t)
            def _():
                send_scores(0).wait_send()
        else:
            send_scores(k).wait_send()


def solution(mesh):
    nd, nt = mesh.shape["dp"], mesh.shape["tensor"]

    def body(hidden, outgrad, down, inproj, up, outproj, tests):
        rows, hid = hidden.shape
        feat = outgrad.shape[1]
        rank, kdim = down.shape[0], inproj.shape[0]
        seqs = rows // LEN
        block = LEN // nt
        tests_here, width = tests.shape
        per = nd // nt
        f32, bf16 = jnp.float32, jnp.bfloat16
        lanes = 2 * kdim
        rep = kdim // rank
        dma = pltpu.SemaphoreType.DMA
        return pl.pallas_call(
            functools.partial(kernel, (nd, nt)),
            out_shape=jax.ShapeDtypeStruct((seqs, tests_here * per), f32),
            in_specs=[pl.BlockSpec(memory_space=pl.ANY)] * 7,
            out_specs=pl.BlockSpec(memory_space=pltpu.VMEM),
            scratch_shapes=[
                pltpu.VMEM((rows, hid), bf16),
                pltpu.VMEM((rows, feat), bf16),
                pltpu.VMEM((lanes, hid), bf16),
                pltpu.VMEM((lanes, feat), bf16),
                pltpu.VMEM((tests_here, width), bf16),
                pltpu.VMEM((seqs, LEN, lanes), f32),
                pltpu.VMEM((seqs, nt, 16, lanes), f32),
                pltpu.VMEM((seqs, nt, block + 32, lanes), WIRE),
                pltpu.VMEM((seqs, nt - 1, block + 32, lanes), WIRE),
                pltpu.VMEM((seqs, rank, lanes), f32),
                pltpu.VMEM((nt - 1, seqs, rank, lanes), f32),
                pltpu.VMEM((8, width), f32),
                pltpu.VMEM((nd - 1, 8, width), f32),
                pltpu.VMEM((nd, 8, tests_here), f32),
                pltpu.VMEM((per, nt, 8, tests_here), f32),
                dma((seqs,)), dma((seqs,)), dma((2 + 2 * rep,)), dma,
                dma((seqs, nt - 1)), dma((seqs, nt - 1)),
                dma((seqs, nt - 1)), dma((seqs, nt - 1)),
                dma((nd - 1,)), dma((nd - 1,)),
                dma((nd,)), dma((per, nt)),
            ],
            compiler_params=pltpu.CompilerParams(
                collective_id=0, has_side_effects=True, vmem_limit_bytes=56 * 1024 * 1024,
            ),
            cost_estimate=pl.CostEstimate(
                flops=2 * rows * (hid + feat) * lanes,
                bytes_accessed=2 * rows * (hid + feat), transcendentals=0,
            ),
        )(hidden, outgrad, down, inproj, up.T, outproj, tests)

    return jax.shard_map(
        body,
        mesh=mesh,
        in_specs=(
            P(("parts", "dp"), "tensor"),
            P(("parts", "dp"), "tensor"),
            P(None, "tensor"),
            P(None, "tensor"),
            P("tensor", None),
            P(None, "tensor"),
            P("dp", "tensor"),
        ),
        out_specs=P(("parts", "dp"), "tensor"),
        check_vma=False,
    )
```

```python
import functools

import jax
import jax.numpy as jnp
from jax import lax
from jax.experimental import pallas as pl
from jax.experimental.pallas import tpu as pltpu
from jax.sharding import PartitionSpec as P

LEN = 256
PIECES = 3
AHEAD = 3
MESH = pl.DeviceIdType.MESH
WIRE = jnp.bfloat16
CONTRACT_LAST = (((1,), (1,)), ((), ()))
CONTRACT_FIRST = (((0,), (0,)), ((), ()))


def split(x):
    high = x.astype(jnp.bfloat16)
    return jnp.concatenate([high, (x - high.astype(jnp.float32)).astype(jnp.bfloat16)], 0)


def kernel(
    sizes,
    hidden, outgrad, down, inproj, up_t, outproj, tests,
    out,
    hid_v, grad_v, left_v, right_v, tests_v,
    own_a, own_b, send_p, recv_p, own_e, recv_e, own_s, all_s, part_s, recv_s,
    hid_sem, grad_sem, w_sem, t_sem,
    p_send, p_recv, e_send, e_recv, s_send, s_recv, o_send, o_recv,
):
    nd, nt = sizes
    rank, kdim = down.shape[0], inproj.shape[0]
    seqs = hidden.shape[0] // LEN
    block = LEN // nt
    pack = min(4, block // 16)
    width = tests.shape[1]
    rep = kdim // rank
    f32, bf16 = jnp.float32, jnp.bfloat16

    part = lax.axis_index("parts")
    d = lax.axis_index("dp")
    t = lax.axis_index("tensor")

    loads = []

    def load(src, dst, sem):
        copy = pltpu.make_async_copy(src, dst, sem)
        copy.start()
        return copy

    w_loads = [
        load(inproj, left_v.at[pl.ds(0, kdim)], w_sem.at[0]),
        load(down, left_v.at[pl.ds(kdim, rank)], w_sem.at[1]),
    ]
    hid = hidden.shape[1]
    cut = hid // (PIECES - 1)
    pieces = []
    for s in range(seqs):
        rows = pl.ds(s * LEN, LEN)
        for i in range(PIECES - 1):
            cols = pl.ds(i * cut, cut)
            pieces.append((hidden.at[rows, cols], hid_v.at[rows, cols], hid_sem.at[s, i]))
        pieces.append((outgrad.at[rows], grad_v.at[rows], grad_sem.at[s]))
    pieces.append((tests, tests_v, t_sem))
    reads = []

    def read_next():
        if len(reads) < len(pieces):
            reads.append(load(*pieces[len(reads)]))

    def arrive(n):
        reads[n].wait()
        read_next()

    for i in range(AHEAD):
        read_next()
        if i == 0:
            w_loads.append(load(up_t, right_v.at[pl.ds(0, rank)], w_sem.at[2]))
            w_loads.append(load(outproj, right_v.at[pl.ds(kdim, kdim)], w_sem.at[3]))

    barrier = pltpu.get_barrier_semaphore()
    for kd in range(nd):
        for kt in range(nt):
            if kd or kt:
                pl.semaphore_signal(
                    barrier, inc=1,
                    device_id=(part, lax.rem(d + kd, nd), lax.rem(t + kt, nt)),
                    device_id_type=MESH,
                )

    lane = lax.broadcasted_iota(jnp.int32, (LEN, 2 * kdim), 1)
    low = lane < kdim
    lane16 = lax.broadcasted_iota(jnp.int32, (16, 2 * kdim), 1)
    group = (lane16 // rank) % rep

    p_copies, e_copies = [], []

    def project(s):
        rows = pl.ds(s * LEN, LEN)
        if s == 0:
            for c in w_loads[:2]:
                c.wait()
            for i in range(1, rep):
                left_v[pl.ds(kdim + rank * i, rank), :] = left_v[pl.ds(kdim, rank), :]
        from_in = None
        for i in range(PIECES - 1):
            cols = pl.ds(i * cut, cut)
            arrive(s * PIECES + i)
            term = lax.dot_general(hid_v[rows, cols], left_v[:, cols], CONTRACT_LAST, preferred_element_type=f32)
            from_in = term if from_in is None else from_in + term
        arrive(s * PIECES + PIECES - 1)
        if s == 0:
            for c in w_loads[2:]:
                c.wait()
            for i in range(1, rep):
                right_v[pl.ds(rank * i, rank), :] = right_v[pl.ds(0, rank), :]
        from_gr = lax.dot_general(grad_v[rows, :], right_v[...], CONTRACT_LAST, preferred_element_type=f32)
        a = jnp.where(low, from_in, from_gr)
        b = jnp.where(low, from_gr, from_in)
        own_a[s] = a
        for j in range(nt):
            at = j * block
            packed = jnp.zeros((16, 2 * kdim), f32)
            for i in range(pack):
                packed = jnp.where(group == i, b[at + 16 * i:at + 16 * i + 16], packed)
            own_b[s, j] = packed
            send_p[s, j, pl.ds(0, block), :] = a[at:at + block].astype(WIRE)
            packed_hi = packed.astype(WIRE)
            send_p[s, j, pl.ds(block, 16), :] = packed_hi
            send_p[s, j, pl.ds(block + 16, 16), :] = (packed - packed_hi.astype(f32)).astype(WIRE)
        if s == 0:
            pl.semaphore_wait(barrier, nd * nt - 1)
        copies = []
        for k in range(1, nt):
            to = lax.rem(t + k, nt)
            c = pltpu.make_async_remote_copy(
                src_ref=send_p.at[s, to], dst_ref=recv_p.at[s, k - 1],
                send_sem=p_send.at[s, k - 1], recv_sem=p_recv.at[s, k - 1],
                device_id=(part, d, to), device_id_type=MESH,
            )
            c.start()
            copies.append(c)
        p_copies.append(copies)

    def bilinear(s):
        for c in p_copies[s]:
            c.wait_recv()
        a = own_a[s, pl.ds(pl.multiple_of(t * block, block), block), :]
        b = own_b[s, t]
        for k in range(nt - 1):
            a = a + recv_p[s, k, pl.ds(0, block), :].astype(f32)
            b = b + recv_p[s, k, pl.ds(block, 16), :].astype(f32)
            b = b + recv_p[s, k, pl.ds(block + 16, 16), :].astype(f32)
        b = jnp.concatenate([jnp.where(group == i, b, 0.0) for i in range(pack)], 0)
        a_hi, b_hi = a.astype(bf16), b.astype(bf16)
        a_lo = (a - a_hi.astype(f32)).astype(bf16)
        b_lo = (b - b_hi.astype(f32)).astype(bf16)
        z = lax.dot_general(
            jnp.concatenate([b_hi, b_lo, b_hi], 0), jnp.concatenate([a_hi, a_hi, a_lo], 0),
            CONTRACT_FIRST, preferred_element_type=f32,
        )
        va, ub = z[0:rank], z[kdim:kdim + rank]
        for i in range(1, pack):
            va = va + z[rank * i:rank * i + rank]
            ub = ub + z[kdim + rank * i:kdim + rank * i + rank]
        own_e[s] = jnp.where(lane16 < kdim, va, ub)
        copies = []
        for k in range(1, nt):
            to = lax.rem(t + k, nt)
            c = pltpu.make_async_remote_copy(
                src_ref=own_e.at[s], dst_ref=recv_e.at[k - 1, s],
                send_sem=e_send.at[s, k - 1], recv_sem=e_recv.at[s, k - 1],
                device_id=(part, d, to), device_id_type=MESH,
            )
            c.start()
            copies.append(c)
        e_copies.append(copies)

    for s in range(seqs):
        project(s)
        if s >= 2:
            bilinear(s - 2)
    for s in range(max(seqs - 2, 0), seqs):
        bilinear(s)

    half = rank * kdim
    rows_e = 2 * seqs * rank
    col = lax.broadcasted_iota(jnp.int32, (2 * kdim, width), 1) + t * width
    lane_of = jnp.where(col < half, kdim + col // rank, (col - half) % kdim)
    pick = (lax.broadcasted_iota(jnp.int32, (2 * kdim, width), 0) == lane_of).astype(bf16)
    colr = lax.broadcasted_iota(jnp.int32, (rows_e, width), 1) + t * width
    row_of = jnp.where(colr < half, colr % rank, (colr - half) // kdim)
    keep = (lax.broadcasted_iota(jnp.int32, (rows_e, width), 0) % rank) == row_of
    fold = (
        (lax.broadcasted_iota(jnp.int32, (8, rows_e), 1) // rank) % seqs
        == lax.broadcasted_iota(jnp.int32, (8, rows_e), 0)
    ).astype(bf16)

    for copies in e_copies:
        for c in copies:
            c.wait_recv()
    e = own_e[...]
    for k in range(nt - 1):
        e = e + recv_e[k]
    e = split(e.reshape(seqs * rank, 2 * kdim))
    spread = jnp.dot(e, pick, preferred_element_type=f32)
    spread = jnp.where(keep, spread, 0.0).astype(bf16)
    example = jnp.dot(fold, spread, preferred_element_type=f32)
    own_s[...] = example
    s_copies = []
    for k in range(1, nd):
        c = pltpu.make_async_remote_copy(
            src_ref=own_s, dst_ref=all_s.at[k - 1],
            send_sem=s_send.at[k - 1], recv_sem=s_recv.at[k - 1],
            device_id=(part, lax.rem(d + k, nd), t), device_id_type=MESH,
        )
        c.start()
        s_copies.append(c)
    reads[-1].wait()

    for c in s_copies:
        c.wait_recv()
    stacked = split(jnp.concatenate([example] + [all_s[k] for k in range(nd - 1)], 0))
    scores = lax.dot_general(stacked, tests_v[...], CONTRACT_LAST, preferred_element_type=f32)
    scores = scores[:8 * nd] + scores[8 * nd:]
    per = nd // nt
    home = d // per
    slot = lax.rem(d, per)
    part_s[...] = scores.reshape(part_s.shape)

    def send_scores(k):
        to = lax.rem(d + nd - k, nd)
        return pltpu.make_async_remote_copy(
            src_ref=part_s.at[k, pl.ds(0, seqs)], dst_ref=recv_s.at[slot, t, pl.ds(0, seqs)],
            send_sem=o_send.at[k], recv_sem=o_recv.at[slot, t],
            device_id=(part, to, home), device_id_type=MESH,
        )

    for k in range(nd):
        if k == 0:
            @pl.when(home != t)
            def _():
                send_scores(0).start()

            @pl.when(home == t)
            def _():
                recv_s[slot, t, pl.ds(0, seqs), :] = part_s[0, pl.ds(0, seqs), :]
        else:
            send_scores(k).start()

    for j in range(per):
        total = None
        for i in range(nt):
            local = jnp.logical_and(t * per + j == d, i == t)

            @pl.when(jnp.logical_not(local))
            def _():
                pltpu.make_async_remote_copy(
                    src_ref=part_s.at[0, pl.ds(0, seqs)], dst_ref=recv_s.at[j, i, pl.ds(0, seqs)],
                    send_sem=o_send.at[0], recv_sem=o_recv.at[j, i],
                    device_id=(part, d, t), device_id_type=MESH,
                ).wait_recv()
            here = recv_s[j, i, pl.ds(0, seqs), :]
            total = here if total is None else total + here
        tests_here = tests.shape[0]
        out[:, j * tests_here:(j + 1) * tests_here] = total

    for copies in p_copies + e_copies + [s_copies]:
        for c in copies:
            c.wait_send()
    for k in range(nd):
        if k == 0:
            @pl.when(home != t)
            def _():
                send_scores(0).wait_send()
        else:
            send_scores(k).wait_send()


def solution(mesh):
    nd, nt = mesh.shape["dp"], mesh.shape["tensor"]

    def body(hidden, outgrad, down, inproj, up, outproj, tests):
        rows, hid = hidden.shape
        feat = outgrad.shape[1]
        rank, kdim = down.shape[0], inproj.shape[0]
        seqs = rows // LEN
        block = LEN // nt
        tests_here, width = tests.shape
        per = nd // nt
        f32, bf16 = jnp.float32, jnp.bfloat16
        lanes = 2 * kdim
        rep = kdim // rank
        dma = pltpu.SemaphoreType.DMA
        return pl.pallas_call(
            functools.partial(kernel, (nd, nt)),
            out_shape=jax.ShapeDtypeStruct((seqs, tests_here * per), f32),
            in_specs=[pl.BlockSpec(memory_space=pl.ANY)] * 7,
            out_specs=pl.BlockSpec(memory_space=pltpu.VMEM),
            scratch_shapes=[
                pltpu.VMEM((rows, hid), bf16),
                pltpu.VMEM((rows, feat), bf16),
                pltpu.VMEM((lanes, hid), bf16),
                pltpu.VMEM((lanes, feat), bf16),
                pltpu.VMEM((tests_here, width), bf16),
                pltpu.VMEM((seqs, LEN, lanes), f32),
                pltpu.VMEM((seqs, nt, 16, lanes), f32),
                pltpu.VMEM((seqs, nt, block + 32, lanes), WIRE),
                pltpu.VMEM((seqs, nt - 1, block + 32, lanes), WIRE),
                pltpu.VMEM((seqs, rank, lanes), f32),
                pltpu.VMEM((nt - 1, seqs, rank, lanes), f32),
                pltpu.VMEM((8, width), f32),
                pltpu.VMEM((nd - 1, 8, width), f32),
                pltpu.VMEM((nd, 8, tests_here), f32),
                pltpu.VMEM((per, nt, 8, tests_here), f32),
                dma((seqs, PIECES - 1)), dma((seqs,)), dma((4,)), dma,
                dma((seqs, nt - 1)), dma((seqs, nt - 1)),
                dma((seqs, nt - 1)), dma((seqs, nt - 1)),
                dma((nd - 1,)), dma((nd - 1,)),
                dma((nd,)), dma((per, nt)),
            ],
            compiler_params=pltpu.CompilerParams(
                collective_id=0, has_side_effects=True, vmem_limit_bytes=56 * 1024 * 1024,
            ),
            cost_estimate=pl.CostEstimate(
                flops=2 * rows * (hid + feat) * lanes,
                bytes_accessed=2 * rows * (hid + feat), transcendentals=0,
            ),
        )(hidden, outgrad, down, inproj, up.T, outproj, tests)

    return jax.shard_map(
        body,
        mesh=mesh,
        in_specs=(
            P(("parts", "dp"), "tensor"),
            P(("parts", "dp"), "tensor"),
            P(None, "tensor"),
            P(None, "tensor"),
            P("tensor", None),
            P(None, "tensor"),
            P("dp", "tensor"),
        ),
        out_specs=P(("parts", "dp"), "tensor"),
        check_vma=False,
    )
```

```python
import functools

import jax
import jax.numpy as jnp
from jax import lax
from jax.experimental import pallas as pl
from jax.experimental.pallas import tpu as pltpu
from jax.sharding import PartitionSpec as P

LEN = 256
PIECES = 2
AHEAD = 4
MESH = pl.DeviceIdType.MESH
WIRE = jnp.bfloat16
CONTRACT_LAST = (((1,), (1,)), ((), ()))
CONTRACT_FIRST = (((0,), (0,)), ((), ()))


def split(x):
    high = x.astype(jnp.bfloat16)
    return jnp.concatenate([high, (x - high.astype(jnp.float32)).astype(jnp.bfloat16)], 0)


def kernel(
    sizes,
    hidden, outgrad, down, inproj, up_t, outproj, tests,
    out,
    hid_v, grad_v, left_v, right_v, tests_v,
    own_a, own_b, send_p, recv_p, own_e, recv_e, own_s, all_s, part_s, recv_s,
    hid_sem, grad_sem, w_sem, t_sem,
    p_send, p_recv, e_send, e_recv, s_send, s_recv, o_send, o_recv,
):
    nd, nt = sizes
    rank, kdim = down.shape[0], inproj.shape[0]
    seqs = hidden.shape[0] // LEN
    block = LEN // nt
    pack = min(4, block // 16)
    width = tests.shape[1]
    rep = kdim // rank
    f32, bf16 = jnp.float32, jnp.bfloat16

    part = lax.axis_index("parts")
    d = lax.axis_index("dp")
    t = lax.axis_index("tensor")

    loads = []

    def load(src, dst, sem):
        copy = pltpu.make_async_copy(src, dst, sem)
        copy.start()
        return copy

    w_loads = [
        load(inproj, left_v.at[pl.ds(0, kdim)], w_sem.at[0]),
        load(down, left_v.at[pl.ds(kdim, rank)], w_sem.at[1]),
    ]
    hid = hidden.shape[1]
    cut = hid // (PIECES - 1)
    pieces = []
    for s in range(seqs):
        rows = pl.ds(s * LEN, LEN)
        for i in range(PIECES - 1):
            cols = pl.ds(i * cut, cut)
            pieces.append((hidden.at[rows, cols], hid_v.at[rows, cols], hid_sem.at[s, i]))
        pieces.append((outgrad.at[rows], grad_v.at[rows], grad_sem.at[s]))
    pieces.append((tests, tests_v, t_sem))
    reads = []

    def read_next():
        if len(reads) < len(pieces):
            reads.append(load(*pieces[len(reads)]))

    def arrive(n):
        reads[n].wait()
        read_next()

    for i in range(AHEAD):
        read_next()
        if i == 0:
            w_loads.append(load(up_t, right_v.at[pl.ds(0, rank)], w_sem.at[2]))
            w_loads.append(load(outproj, right_v.at[pl.ds(kdim, kdim)], w_sem.at[3]))

    barrier = pltpu.get_barrier_semaphore()
    for kd in range(nd):
        for kt in range(nt):
            if kd or kt:
                pl.semaphore_signal(
                    barrier, inc=1,
                    device_id=(part, lax.rem(d + kd, nd), lax.rem(t + kt, nt)),
                    device_id_type=MESH,
                )

    lane = lax.broadcasted_iota(jnp.int32, (LEN, 2 * kdim), 1)
    low = lane < kdim
    lane16 = lax.broadcasted_iota(jnp.int32, (16, 2 * kdim), 1)
    group = (lane16 // rank) % rep

    p_copies, e_copies = [], []

    def project(s):
        rows = pl.ds(s * LEN, LEN)
        if s == 0:
            for c in w_loads[:2]:
                c.wait()
            for i in range(1, rep):
                left_v[pl.ds(kdim + rank * i, rank), :] = left_v[pl.ds(kdim, rank), :]
        from_in = None
        for i in range(PIECES - 1):
            cols = pl.ds(i * cut, cut)
            arrive(s * PIECES + i)
            term = lax.dot_general(hid_v[rows, cols], left_v[:, cols], CONTRACT_LAST, preferred_element_type=f32)
            from_in = term if from_in is None else from_in + term
        arrive(s * PIECES + PIECES - 1)
        if s == 0:
            for c in w_loads[2:]:
                c.wait()
            for i in range(1, rep):
                right_v[pl.ds(rank * i, rank), :] = right_v[pl.ds(0, rank), :]
        from_gr = lax.dot_general(grad_v[rows, :], right_v[...], CONTRACT_LAST, preferred_element_type=f32)
        a = jnp.where(low, from_in, from_gr)
        b = jnp.where(low, from_gr, from_in)
        own_a[s] = a
        for j in range(nt):
            at = j * block
            packed = jnp.zeros((16, 2 * kdim), f32)
            for i in range(pack):
                packed = jnp.where(group == i, b[at + 16 * i:at + 16 * i + 16], packed)
            own_b[s, j] = packed
            send_p[s, j, pl.ds(0, block), :] = a[at:at + block].astype(WIRE)
            packed_hi = packed.astype(WIRE)
            send_p[s, j, pl.ds(block, 16), :] = packed_hi
            send_p[s, j, pl.ds(block + 16, 16), :] = (packed - packed_hi.astype(f32)).astype(WIRE)
        if s == 0:
            pl.semaphore_wait(barrier, nd * nt - 1)
        copies = []
        for k in range(1, nt):
            to = lax.rem(t + k, nt)
            c = pltpu.make_async_remote_copy(
                src_ref=send_p.at[s, to], dst_ref=recv_p.at[s, k - 1],
                send_sem=p_send.at[s, k - 1], recv_sem=p_recv.at[s, k - 1],
                device_id=(part, d, to), device_id_type=MESH,
            )
            c.start()
            copies.append(c)
        p_copies.append(copies)

    def bilinear(s):
        for c in p_copies[s]:
            c.wait_recv()
        a = own_a[s, pl.ds(pl.multiple_of(t * block, block), block), :]
        b = own_b[s, t]
        for k in range(nt - 1):
            a = a + recv_p[s, k, pl.ds(0, block), :].astype(f32)
            b = b + recv_p[s, k, pl.ds(block, 16), :].astype(f32)
            b = b + recv_p[s, k, pl.ds(block + 16, 16), :].astype(f32)
        b = jnp.concatenate([jnp.where(group == i, b, 0.0) for i in range(pack)], 0)
        a_hi, b_hi = a.astype(bf16), b.astype(bf16)
        a_lo = (a - a_hi.astype(f32)).astype(bf16)
        b_lo = (b - b_hi.astype(f32)).astype(bf16)
        z = lax.dot_general(
            jnp.concatenate([b_hi, b_lo, b_hi], 0), jnp.concatenate([a_hi, a_hi, a_lo], 0),
            CONTRACT_FIRST, preferred_element_type=f32,
        )
        va, ub = z[0:rank], z[kdim:kdim + rank]
        for i in range(1, pack):
            va = va + z[rank * i:rank * i + rank]
            ub = ub + z[kdim + rank * i:kdim + rank * i + rank]
        own_e[s] = jnp.where(lane16 < kdim, va, ub)
        copies = []
        for k in range(1, nt):
            to = lax.rem(t + k, nt)
            c = pltpu.make_async_remote_copy(
                src_ref=own_e.at[s], dst_ref=recv_e.at[k - 1, s],
                send_sem=e_send.at[s, k - 1], recv_sem=e_recv.at[s, k - 1],
                device_id=(part, d, to), device_id_type=MESH,
            )
            c.start()
            copies.append(c)
        e_copies.append(copies)

    for s in range(seqs):
        project(s)
        if s >= 3:
            bilinear(s - 3)
    for s in range(max(seqs - 3, 0), seqs):
        bilinear(s)

    half = rank * kdim
    rows_e = 2 * seqs * rank
    col = lax.broadcasted_iota(jnp.int32, (2 * kdim, width), 1) + t * width
    lane_of = jnp.where(col < half, kdim + col // rank, (col - half) % kdim)
    pick = (lax.broadcasted_iota(jnp.int32, (2 * kdim, width), 0) == lane_of).astype(bf16)
    colr = lax.broadcasted_iota(jnp.int32, (rows_e, width), 1) + t * width
    row_of = jnp.where(colr < half, colr % rank, (colr - half) // kdim)
    keep = (lax.broadcasted_iota(jnp.int32, (rows_e, width), 0) % rank) == row_of
    fold = (
        (lax.broadcasted_iota(jnp.int32, (8, rows_e), 1) // rank) % seqs
        == lax.broadcasted_iota(jnp.int32, (8, rows_e), 0)
    ).astype(bf16)

    for copies in e_copies:
        for c in copies:
            c.wait_recv()
    e = own_e[...]
    for k in range(nt - 1):
        e = e + recv_e[k]
    e = split(e.reshape(seqs * rank, 2 * kdim))
    spread = jnp.dot(e, pick, preferred_element_type=f32)
    spread = jnp.where(keep, spread, 0.0).astype(bf16)
    example = jnp.dot(fold, spread, preferred_element_type=f32)
    own_s[...] = example
    s_copies = []
    for k in range(1, nd):
        c = pltpu.make_async_remote_copy(
            src_ref=own_s, dst_ref=all_s.at[k - 1],
            send_sem=s_send.at[k - 1], recv_sem=s_recv.at[k - 1],
            device_id=(part, lax.rem(d + k, nd), t), device_id_type=MESH,
        )
        c.start()
        s_copies.append(c)
    reads[-1].wait()

    for c in s_copies:
        c.wait_recv()
    stacked = split(jnp.concatenate([example] + [all_s[k] for k in range(nd - 1)], 0))
    scores = lax.dot_general(stacked, tests_v[...], CONTRACT_LAST, preferred_element_type=f32)
    scores = scores[:8 * nd] + scores[8 * nd:]
    per = nd // nt
    home = d // per
    slot = lax.rem(d, per)
    part_s[...] = scores.reshape(part_s.shape)

    def send_scores(k):
        to = lax.rem(d + nd - k, nd)
        return pltpu.make_async_remote_copy(
            src_ref=part_s.at[k, pl.ds(0, seqs)], dst_ref=recv_s.at[slot, t, pl.ds(0, seqs)],
            send_sem=o_send.at[k], recv_sem=o_recv.at[slot, t],
            device_id=(part, to, home), device_id_type=MESH,
        )

    for k in range(nd):
        if k == 0:
            @pl.when(home != t)
            def _():
                send_scores(0).start()

            @pl.when(home == t)
            def _():
                recv_s[slot, t, pl.ds(0, seqs), :] = part_s[0, pl.ds(0, seqs), :]
        else:
            send_scores(k).start()

    for j in range(per):
        total = None
        for i in range(nt):
            local = jnp.logical_and(t * per + j == d, i == t)

            @pl.when(jnp.logical_not(local))
            def _():
                pltpu.make_async_remote_copy(
                    src_ref=part_s.at[0, pl.ds(0, seqs)], dst_ref=recv_s.at[j, i, pl.ds(0, seqs)],
                    send_sem=o_send.at[0], recv_sem=o_recv.at[j, i],
                    device_id=(part, d, t), device_id_type=MESH,
                ).wait_recv()
            here = recv_s[j, i, pl.ds(0, seqs), :]
            total = here if total is None else total + here
        tests_here = tests.shape[0]
        out[:, j * tests_here:(j + 1) * tests_here] = total

    for copies in p_copies + e_copies + [s_copies]:
        for c in copies:
            c.wait_send()
    for k in range(nd):
        if k == 0:
            @pl.when(home != t)
            def _():
                send_scores(0).wait_send()
        else:
            send_scores(k).wait_send()


def solution(mesh):
    nd, nt = mesh.shape["dp"], mesh.shape["tensor"]

    def body(hidden, outgrad, down, inproj, up, outproj, tests):
        rows, hid = hidden.shape
        feat = outgrad.shape[1]
        rank, kdim = down.shape[0], inproj.shape[0]
        seqs = rows // LEN
        block = LEN // nt
        tests_here, width = tests.shape
        per = nd // nt
        f32, bf16 = jnp.float32, jnp.bfloat16
        lanes = 2 * kdim
        rep = kdim // rank
        dma = pltpu.SemaphoreType.DMA
        return pl.pallas_call(
            functools.partial(kernel, (nd, nt)),
            out_shape=jax.ShapeDtypeStruct((seqs, tests_here * per), f32),
            in_specs=[pl.BlockSpec(memory_space=pl.ANY)] * 7,
            out_specs=pl.BlockSpec(memory_space=pltpu.VMEM),
            scratch_shapes=[
                pltpu.VMEM((rows, hid), bf16),
                pltpu.VMEM((rows, feat), bf16),
                pltpu.VMEM((lanes, hid), bf16),
                pltpu.VMEM((lanes, feat), bf16),
                pltpu.VMEM((tests_here, width), bf16),
                pltpu.VMEM((seqs, LEN, lanes), f32),
                pltpu.VMEM((seqs, nt, 16, lanes), f32),
                pltpu.VMEM((seqs, nt, block + 32, lanes), WIRE),
                pltpu.VMEM((seqs, nt - 1, block + 32, lanes), WIRE),
                pltpu.VMEM((seqs, rank, lanes), f32),
                pltpu.VMEM((nt - 1, seqs, rank, lanes), f32),
                pltpu.VMEM((8, width), f32),
                pltpu.VMEM((nd - 1, 8, width), f32),
                pltpu.VMEM((nd, 8, tests_here), f32),
                pltpu.VMEM((per, nt, 8, tests_here), f32),
                dma((seqs, PIECES - 1)), dma((seqs,)), dma((4,)), dma,
                dma((seqs, nt - 1)), dma((seqs, nt - 1)),
                dma((seqs, nt - 1)), dma((seqs, nt - 1)),
                dma((nd - 1,)), dma((nd - 1,)),
                dma((nd,)), dma((per, nt)),
            ],
            compiler_params=pltpu.CompilerParams(
                collective_id=0, has_side_effects=True, vmem_limit_bytes=56 * 1024 * 1024,
            ),
            cost_estimate=pl.CostEstimate(
                flops=2 * rows * (hid + feat) * lanes,
                bytes_accessed=2 * rows * (hid + feat), transcendentals=0,
            ),
        )(hidden, outgrad, down, inproj, up.T, outproj, tests)

    return jax.shard_map(
        body,
        mesh=mesh,
        in_specs=(
            P(("parts", "dp"), "tensor"),
            P(("parts", "dp"), "tensor"),
            P(None, "tensor"),
            P(None, "tensor"),
            P("tensor", None),
            P(None, "tensor"),
            P("dp", "tensor"),
        ),
        out_specs=P(("parts", "dp"), "tensor"),
        check_vma=False,
    )
```
